32 devices in a mesh: row: 8 (over z, x), col: 4 (over y, core).
Axes of the slice: x: 2, y: 2, z: 4, core: 2. Of those that a mesh axis runs over, the one named last changes fastest.
Arguments:
- amplitudes: bfloat16 [4096, 2048], P('row', 'col'), may hold values from -6 to 6
- integrals: bfloat16 [2048, 2048], P('col', 'row'), may hold values from -0.1875 to 0.1875
- base_residual: float32 [4096, 2048], P('row', 'col'), may hold values from -6 to 6
- inv_denominators: float32 [4096, 2048], P('row', 'col'), may hold values from 0.1 to 0.5
- amp_mask: int32 [16, 8], P('row', 'col'), may hold values 0 or 1
- int_mask: int32 [8, 8], P('col', 'row'), may hold values 0 or 1
- res_mask: int32 [16, 8], P('row', 'col'), may hold values 0 or 1
Outputs:
- new_amplitudes: bfloat16 [4096, 2048], P('row', 'col')
- residual: float32 [4096, 2048], P('row', 'col')
The draws below stay inside these ranges and needn't reach their ends.
Inputs may be any that keep to these rules, and one draw needn't show every extreme that they name: `amp_mask`: tile kept (1) or dropped (0). `int_mask`: tile kept (1) or dropped (0). `res_mask`: tile kept (1) or dropped (0).
All inputs are finite; a program needn't handle non-finite values. No bound on the sum of `amp_mask` or of `int_mask` or of `res_mask` on one device may be relied on, other than what follows from the above.
Results may differ from the reference program's by a relative error of at most 0.012.
Values may be sent and summed in bfloat16 or wider, within the bound.
A program may use at most 128 MiB of HBM per device.

```python
import math
import jax
import jax.numpy as jnp
from jax import lax

B = 256
ITERS = 2
NI = 4096
NK = 2048
N_COL = 4


def touch_ends(array, own_key, least, largest):
    longest = array.shape.index(max(array.shape))
    spots = []
    for shift in (0, 1):
        where = [jax.random.randint(jax.random.fold_in(own_key, axis), (), 0, length) for axis, length in enumerate(array.shape)]
        where[longest] = (where[longest] + shift) % array.shape[longest]
        spots.append(tuple(where))
    return array.at[spots[0]].set(least).at[spots[1]].set(largest)


def strengthened(values, own_key, source, target, parts, factor):
    def block_of(dim):
        return (jnp.arange(values.shape[dim]) // (values.shape[dim] // parts)).reshape((-1,) + (1,) * (values.ndim - 1 - dim))

    near = jax.random.permutation(own_key, parts)[block_of(target)]
    far = (block_of(target) + parts // 2) % parts
    return jnp.where((block_of(source) == near) | (block_of(source) == far), factor * values, values)


def block_levels(rng, dims, cuts, smallest, high):
    factor_of, own = 1.0, jax.random.fold_in(rng, 6)
    for dim, shards_of in cuts:
        steps = jnp.exp(jax.random.uniform(jax.random.fold_in(own, dim), (shards_of,), jnp.float32, smallest / len(cuts), high / len(cuts)))
        factor_of = factor_of * jnp.repeat(steps, dims[dim] // shards_of).reshape([-1 if axis == dim else 1 for axis in range(len(dims))])
    return factor_of


def bell_draw(rng, dims, scale, reach, pieces=(), kind=jnp.bfloat16):
    drawn = scale * jax.random.normal(rng, dims, jnp.float32)
    if pieces:
        drawn = drawn * block_levels(rng, dims, pieces, -0.22, 0.18)
    return jnp.clip(drawn, -reach, reach).astype(kind)


def heavy_noise(key, extent, spread, bound, split, heavy, held_as=jnp.bfloat16):
    drawn = spread * jax.random.normal(key, extent, jnp.float32)
    if split:
        drawn = drawn * block_levels(key, extent, split, -0.22, 0.18)
    return jnp.clip(strengthened(drawn, jax.random.fold_in(key, 3), *heavy), -bound, bound).astype(held_as)


def setup_inputs(seed: int = 0) -> dict:
    seeds = jax.random.split(jax.random.key(seed), 8)
    return {
        "amplitudes": bell_draw(seeds[0], (NI, NK), 1.0, 6.0, ((0, 8), (1, 4))),
        "integrals": heavy_noise(seeds[1], (NK, NK), NK ** -0.5, 0.1875, ((0, 4), (1, 8)), (0, 1, 8, 2.0)),
        "base_residual": bell_draw(seeds[2], (NI, NK), 1.0, 6.0, ((0, 8), (1, 4)), jnp.float32),
        "inv_denominators": jnp.clip(jnp.exp(math.log(0.5) - 1.609438 * jax.random.uniform(seeds[3], (NI, NK), jnp.float32) ** block_levels(seeds[3], (NI, NK), ((0, 8), (1, 4)), -0.2, 0.2)), 0.1, 0.5),
        "amp_mask": touch_ends((jax.random.randint(seeds[4], (NI // B, NK // B), 0, 4) < 3).astype(jnp.int32), jax.random.fold_in(seeds[4], 1), 0, 1),
        "int_mask": touch_ends((jax.random.randint(seeds[5], (NK // B, NK // B), 0, 4) < 3).astype(jnp.int32), jax.random.fold_in(seeds[5], 1), 0, 1),
        "res_mask": touch_ends((jax.random.randint(seeds[6], (NI // B, NK // B), 0, 4) < 3).astype(jnp.int32), jax.random.fold_in(seeds[6], 1), 0, 1),
    }


def expand(block, mask):
    tile_rows, tile_cols = mask.shape
    rows, cols = block.shape
    shaped = block.reshape(tile_rows, rows // tile_rows, tile_cols, cols // tile_cols)
    return (shaped * mask[:, None, :, None].astype(block.dtype)).reshape(rows, cols)


def reference(amplitudes, integrals, base_residual, inv_denominators, amp_mask, int_mask, res_mask):
    masked_ints = expand(integrals, int_mask)
    width = integrals.shape[0] // N_COL
    amps = amplitudes
    residual = base_residual
    for step in range(ITERS):
        masked_amps = expand(amps, amp_mask)

        def add_block(total, index):
            start = (index * width).astype(jnp.int32)
            left = lax.dynamic_slice_in_dim(masked_amps, start, width, 1)
            right = lax.dynamic_slice_in_dim(masked_ints, start, width, 0)
            part = jnp.dot(left, right, preferred_element_type=jnp.float32).astype(jnp.bfloat16)
            part = lax.optimization_barrier(part)
            return total + part.astype(jnp.float32), None

        start_total = jnp.zeros(base_residual.shape, jnp.float32)
        ladder, _ = lax.scan(add_block, start_total, jnp.arange(N_COL, dtype=jnp.int32))
        residual = expand(base_residual + ladder, res_mask)
        amps = (amps.astype(jnp.float32) - inv_denominators * residual).astype(jnp.bfloat16)
    return amps, residual
```

```python
import functools

import jax
import jax.numpy as jnp
from jax import lax
from jax.experimental import pallas as pl
from jax.experimental.pallas import tpu as pltpu
from jax.sharding import PartitionSpec as P

ITERS = 2
MESH = pl.DeviceIdType.MESH


def kernel(
    n_row, n_col,
    amp_mask, int_mask, res_mask, amps_hbm, ints_hbm, base_hbm, inv_hbm,
    new_hbm, res_hbm,
    raw, ints, amps, masked, base, inv, hold, pair_out, pair_in, far_out, far_in, res,
    load_sem, store_sem, up_sem, down_sem, across_sem, ints_sem,
    pair_send, pair_recv, far_send, far_recv,
):
    row, col = lax.axis_index("row"), lax.axis_index("col")
    z, x = row // 2, row % 2
    place, core = col // 2, col % 2
    n_z, n_place = n_row // 2, n_col // 2
    rows, width = amps.shape[0], ints.shape[2]
    pieces = amps.shape[1] // width

    loads = [
        pltpu.make_async_copy(src, dst, load_sem.at[i])
        for i, (src, dst) in enumerate(
            ((ints_hbm, raw), (amps_hbm, amps), (base_hbm, base), (inv_hbm, inv))
        )
    ]
    for load in loads:
        load.start()

    barrier = pltpu.get_barrier_semaphore()

    def greet(r, c):
        pl.semaphore_signal(barrier, inc=1, device_id=(r, c), device_id_type=MESH)

    greet(row, place * 2 + 1 - core)
    greet(z * 2 + 1 - x, col)

    @pl.when(z > 0)
    def _():
        greet(row - 2, col)

    @pl.when(z < n_z - 1)
    def _():
        greet(row + 2, col)

    for t in range(1, n_place):
        greet(row, lax.rem(place + t, n_place) * 2 + core)

    loads[0].wait()
    t_r, t_c = int_mask.shape
    h_r, h_c = raw.shape[0] // t_r, raw.shape[1] // t_c
    for i in range(t_r):
        for j in range(t_c):
            part = (slice(i * h_r, (i + 1) * h_r), slice(j * h_c, (j + 1) * h_c))
            keep = int_mask[i, j].astype(jnp.float32)
            ints[row, part[0], part[1]] = (raw[part].astype(jnp.float32) * keep).astype(ints.dtype)

    peers = n_place + 1 + (z > 0).astype(jnp.int32) + (z < n_z - 1).astype(jnp.int32)
    pl.semaphore_wait(barrier, peers)

    def move(r, send_sem, target):
        return pltpu.make_async_remote_copy(
            src_ref=ints.at[r], dst_ref=ints.at[r], send_sem=send_sem.at[r],
            recv_sem=ints_sem.at[r], device_id=(target, col), device_id_type=MESH,
        )

    def upward(r):
        return move(r, up_sem, row + 2)

    def downward(r):
        return move(r, down_sem, row - 2)

    def across(r):
        return move(r, across_sem, z * 2 + 1 - x)

    def pair_copy(step, q):
        return pltpu.make_async_remote_copy(
            src_ref=pair_out.at[step, q], dst_ref=pair_in.at[step, q],
            send_sem=pair_send.at[step, q], recv_sem=pair_recv.at[step, q],
            device_id=(row, place * 2 + 1 - core), device_id_type=MESH,
        )

    def far_copy(step, owner, h):
        return pltpu.make_async_remote_copy(
            src_ref=far_out.at[step, owner * pieces + h],
            dst_ref=far_in.at[step, place * pieces + h],
            send_sem=far_send.at[step, owner * pieces + h],
            recv_sem=far_recv.at[step, place * pieces + h],
            device_id=(row, owner * 2 + core), device_id_type=MESH,
        )

    def far_arrival(step, source, h):
        return pltpu.make_async_remote_copy(
            src_ref=far_out.at[step, source * pieces + h],
            dst_ref=far_in.at[step, source * pieces + h],
            send_sem=far_send.at[step, source * pieces + h],
            recv_sem=far_recv.at[step, source * pieces + h],
            device_id=(row, source * 2 + core), device_id_type=MESH,
        )

    def multiply(step, r):
        owner = r // pieces
        q = (owner // 2) * pieces + r % pieces
        mine = owner % 2 == core

        @pl.when(mine)
        def _():
            hold[q] = jnp.dot(masked[...], ints[r], preferred_element_type=jnp.float32)

        @pl.when(jnp.logical_not(mine))
        def _():
            pair_out[step, q] = jnp.dot(
                masked[...], ints[r], preferred_element_type=jnp.float32
            ).astype(pair_out.dtype)
            pair_copy(step, q).start()

    def combine(step, r):
        owner = r // pieces
        q = (owner // 2) * pieces + r % pieces

        @pl.when(owner % 2 == core)
        def _():
            pair_copy(step, q).wait_recv()

            @pl.when(owner // 2 == place)
            def _():
                hold[q] = hold[q] + pair_in[step, q].astype(jnp.float32)

            @pl.when(owner // 2 != place)
            def _():
                far_out[step, q] = (hold[q] + pair_in[step, q].astype(jnp.float32)).astype(far_out.dtype)
                far_copy(step, owner // 2, r % pieces).start()

    a_r, a_c = amp_mask.shape
    m_r, m_c = rows // a_r, amps.shape[1] // a_c

    def mask_amps():
        for i in range(a_r):
            for j in range(a_c):
                part = (slice(i * m_r, (i + 1) * m_r), slice(j * m_c, (j + 1) * m_c))
                keep = amp_mask[i, j].astype(jnp.float32)
                masked[part] = (amps[part].astype(jnp.float32) * keep).astype(masked.dtype)

    across(row).start()

    @pl.when(z < n_z - 1)
    def _():
        upward(row).start()

    @pl.when(z > 0)
    def _():
        downward(row).start()

    loads[1].wait()
    mask_amps()

    def each_side(distance, act):
        @pl.when((distance >= 0) & (z - distance >= 0))
        def _():
            act(z - distance, 1)

        @pl.when((distance > 0) & (z + distance < n_z))
        def _():
            act(z + distance, -1)

    def gather_step(d, _):
        def arrive(zz, direction):
            r = zz * 2 + x

            @pl.when(d > 0)
            def _():
                across(r).wait_recv()
                across(r).start()
                if direction > 0:
                    @pl.when(z < n_z - 1)
                    def _():
                        upward(r).start()
                else:
                    @pl.when(z > 0)
                    def _():
                        downward(r).start()

        def near(zz, direction):
            multiply(0, zz * 2 + x)

        def other(zz, direction):
            r = zz * 2 + 1 - x
            across(r).wait_recv()
            multiply(0, r)

        each_side(d, arrive)

        @pl.when(d < n_z)
        def _():
            each_side(d, near)

        each_side(d - 1, other)
        each_side(d - 1, lambda zz, direction: combine(0, zz * 2 + x))
        each_side(d - 2, lambda zz, direction: combine(0, zz * 2 + 1 - x))
        return 0

    lax.fori_loop(0, n_z + 2, gather_step, 0)

    loads[2].wait()
    loads[3].wait()
    r_r, r_c = res_mask.shape
    g_r, g_c = rows // r_r, amps.shape[1] // r_c

    def update(step):
        last = step == ITERS - 1
        stores = []
        for h in range(pieces):
            for t in range(1, n_place):
                far_arrival(step, lax.rem(place + t, n_place), h).wait_recv()
            for i in range(r_r):
                for j in range(h * width // g_c, (h + 1) * width // g_c):
                    down = slice(i * g_r, (i + 1) * g_r)
                    along = slice(j * g_c, (j + 1) * g_c)
                    local = slice(j * g_c - h * width, (j + 1) * g_c - h * width)
                    ladder = hold[place * pieces + h, down, local]
                    for t in range(1, n_place):
                        slot = lax.rem(place + t, n_place) * pieces + h
                        ladder = ladder + far_in[step, slot, down, local].astype(jnp.float32)
                    value = (base[down, along] + ladder) * res_mask[i, j].astype(jnp.float32)
                    if last:
                        res[down, along] = value
                    amps[down, along] = (
                        amps[down, along].astype(jnp.float32) - inv[down, along] * value
                    ).astype(amps.dtype)
            if last:
                cut = (slice(None), slice(h * width, (h + 1) * width))
                stores += [
                    pltpu.make_async_copy(amps.at[cut], new_hbm.at[cut], store_sem.at[2 * h]),
                    pltpu.make_async_copy(res.at[cut], res_hbm.at[cut], store_sem.at[2 * h + 1]),
                ]
                stores[-2].start()
                stores[-1].start()
        return stores

    stores = update(0)
    for step in range(1, ITERS):
        mask_amps()

        def place_step(t, _):
            there = lax.rem(place + 1 + t, n_place)
            first = there * 2 * pieces
            for h in range(pieces):
                multiply(step, first + (1 - core) * pieces + h)
            for h in range(pieces):
                multiply(step, first + core * pieces + h)
                combine(step, first + core * pieces + h)
            return 0

        lax.fori_loop(0, n_place, place_step, 0)
        stores = update(step)

    def drain_lines(zz, _):
        r = zz * 2 + x
        across(r).wait_send()

        @pl.when((zz <= z) & (z < n_z - 1))
        def _():
            upward(r).wait_send()

        @pl.when((zz >= z) & (z > 0))
        def _():
            downward(r).wait_send()

        return 0

    lax.fori_loop(0, n_z, drain_lines, 0)
    for step in range(ITERS):
        def drain_pair(q, _):
            pair_copy(step, q).wait_send()
            return 0

        lax.fori_loop(0, n_place * pieces, drain_pair, 0)
        for t in range(1, n_place):
            for h in range(pieces):
                far_copy(step, lax.rem(place + t, n_place), h).wait_send()
    for store in stores:
        store.wait()


def shards(n_row, n_col, amplitudes, integrals, base_residual, inv_denominators, amp_mask, int_mask, res_mask):
    rows, depth = amplitudes.shape
    width = integrals.shape[1]
    pieces = depth // width
    slots = (n_col // 2) * pieces
    any_spec = pl.BlockSpec(memory_space=pl.ANY)
    smem = pl.BlockSpec(memory_space=pltpu.SMEM)
    bf16, f32 = jnp.bfloat16, jnp.float32
    dma = pltpu.SemaphoreType.DMA
    return pl.pallas_call(
        functools.partial(kernel, n_row, n_col),
        out_shape=(
            jax.ShapeDtypeStruct(amplitudes.shape, bf16),
            jax.ShapeDtypeStruct(base_residual.shape, f32),
        ),
        in_specs=[smem] * 3 + [any_spec] * 4,
        out_specs=(any_spec, any_spec),
        scratch_shapes=[
            pltpu.VMEM(integrals.shape, bf16),
            pltpu.VMEM((n_row,) + integrals.shape, bf16),
            pltpu.VMEM((rows, depth), bf16),
            pltpu.VMEM((rows, depth), bf16),
            pltpu.VMEM((rows, depth), f32),
            pltpu.VMEM((rows, depth), f32),
            pltpu.VMEM((slots, rows, width), f32),
            pltpu.VMEM((ITERS, slots, rows, width), bf16),
            pltpu.VMEM((ITERS, slots, rows, width), bf16),
            pltpu.VMEM((ITERS, slots, rows, width), bf16),
            pltpu.VMEM((ITERS, slots, rows, width), bf16),
            pltpu.VMEM((rows, depth), f32),
            dma((4,)), dma((2 * pieces,)),
            dma((n_row,)), dma((n_row,)), dma((n_row,)), dma((n_row,)),
            dma((ITERS, slots)), dma((ITERS, slots)), dma((ITERS, slots)), dma((ITERS, slots)),
        ],
        compiler_params=pltpu.CompilerParams(
            collective_id=0, has_side_effects=True, vmem_limit_bytes=60 * 2**20
        ),
    )(amp_mask, int_mask, res_mask, amplitudes, integrals, base_residual, inv_denominators)


def solution(mesh):
    in_specs = (
        P("row", "col"),
        P("col", "row"),
        P("row", "col"),
        P("row", "col"),
        P("row", "col"),
        P("col", "row"),
        P("row", "col"),
    )
    out_specs = (P("row", "col"), P("row", "col"))
    body = functools.partial(shards, mesh.shape["row"], mesh.shape["col"])
    return jax.shard_map(body, mesh=mesh, in_specs=in_specs, out_specs=out_specs, check_vma=False)
```

```python
import functools

import jax
import jax.numpy as jnp
from jax import lax
from jax.experimental import pallas as pl
from jax.experimental.pallas import tpu as pltpu
from jax.sharding import PartitionSpec as P

ITERS = 2
CUTS = 2
MESH = pl.DeviceIdType.MESH


def kernel(
    n_row, n_col,
    amp_mask, int_mask, res_mask, amps_hbm, ints_hbm, base_hbm, inv_hbm,
    new_hbm, res_hbm,
    raw, ints, amps, masked, base, inv, hold, pair_out, pair_in, far_out, far_in, res,
    load_sem, store_sem, up_sem, down_sem, across_sem, ints_sem,
    pair_send, pair_recv, far_send, far_recv,
):
    row, col = lax.axis_index("row"), lax.axis_index("col")
    z, x = row // 2, row % 2
    place, core = col // 2, col % 2
    n_z, n_place = n_row // 2, n_col // 2
    rows, width = amps.shape[0], ints.shape[2]
    pieces = amps.shape[1] // width

    loads = [
        pltpu.make_async_copy(src, dst, load_sem.at[i])
        for i, (src, dst) in enumerate(
            ((ints_hbm, raw), (amps_hbm, amps), (base_hbm, base), (inv_hbm, inv))
        )
    ]
    for load in loads:
        load.start()

    barrier = pltpu.get_barrier_semaphore()

    def greet(r, c):
        pl.semaphore_signal(barrier, inc=1, device_id=(r, c), device_id_type=MESH)

    greet(row, place * 2 + 1 - core)
    greet(z * 2 + 1 - x, col)

    @pl.when(z > 0)
    def _():
        greet(row - 2, col)

    @pl.when(z < n_z - 1)
    def _():
        greet(row + 2, col)

    for t in range(1, n_place):
        greet(row, lax.rem(place + t, n_place) * 2 + core)

    loads[0].wait()
    t_c, t_r = int_mask.shape
    h_r, h_c = raw.shape[0] // t_r, raw.shape[1] // t_c
    span = min(width, h_c)
    for i in range(t_r):
        for left in range(0, raw.shape[1], span):
            down = slice(i * h_r, (i + 1) * h_r)
            at = left % width
            keep = int_mask[left // h_c, i].astype(jnp.float32)
            ints[row * CUTS + left // width, down, at:at + span] = (
                raw[down, left:left + span].astype(jnp.float32) * keep
            ).astype(ints.dtype)

    peers = n_place + 1 + (z > 0).astype(jnp.int32) + (z < n_z - 1).astype(jnp.int32)
    pl.semaphore_wait(barrier, peers)

    def move(r, send_sem, target):
        return pltpu.make_async_remote_copy(
            src_ref=ints.at[r], dst_ref=ints.at[r], send_sem=send_sem.at[r],
            recv_sem=ints_sem.at[r], device_id=(target, col), device_id_type=MESH,
        )

    def upward(r):
        return move(r, up_sem, row + 2)

    def downward(r):
        return move(r, down_sem, row - 2)

    def across(r):
        return move(r, across_sem, z * 2 + 1 - x)

    def pair_copy(step, q):
        return pltpu.make_async_remote_copy(
            src_ref=pair_out.at[step, q], dst_ref=pair_in.at[step, q],
            send_sem=pair_send.at[step, q], recv_sem=pair_recv.at[step, q],
            device_id=(row, place * 2 + 1 - core), device_id_type=MESH,
        )

    def far_copy(step, owner, h):
        return pltpu.make_async_remote_copy(
            src_ref=far_out.at[step, owner * pieces + h],
            dst_ref=far_in.at[step, place * pieces + h],
            send_sem=far_send.at[step, owner * pieces + h],
            recv_sem=far_recv.at[step, place * pieces + h],
            device_id=(row, owner * 2 + core), device_id_type=MESH,
        )

    def far_arrival(step, source, h):
        return pltpu.make_async_remote_copy(
            src_ref=far_out.at[step, source * pieces + h],
            dst_ref=far_in.at[step, source * pieces + h],
            send_sem=far_send.at[step, source * pieces + h],
            recv_sem=far_recv.at[step, source * pieces + h],
            device_id=(row, source * 2 + core), device_id_type=MESH,
        )

    def multiply(step, r):
        owner = r // pieces
        q = (owner // 2) * pieces + r % pieces
        mine = owner % 2 == core

        @pl.when(mine)
        def _():
            hold[q] = jnp.dot(masked[...], ints[r], preferred_element_type=jnp.float32)

        @pl.when(jnp.logical_not(mine))
        def _():
            pair_out[step, q] = jnp.dot(
                masked[...], ints[r], preferred_element_type=jnp.float32
            ).astype(pair_out.dtype)
            pair_copy(step, q).start()

    def combine(step, r):
        owner = r // pieces
        q = (owner // 2) * pieces + r % pieces

        @pl.when(owner % 2 == core)
        def _():
            pair_copy(step, q).wait_recv()

            @pl.when(owner // 2 == place)
            def _():
                hold[q] = hold[q] + pair_in[step, q].astype(jnp.float32)

            @pl.when(owner // 2 != place)
            def _():
                far_out[step, q] = (hold[q] + pair_in[step, q].astype(jnp.float32)).astype(far_out.dtype)
                far_copy(step, owner // 2, r % pieces).start()

    a_r, a_c = amp_mask.shape
    m_r, m_c = rows // a_r, amps.shape[1] // a_c

    def mask_amps():
        for i in range(a_r):
            for j in range(a_c):
                part = (slice(i * m_r, (i + 1) * m_r), slice(j * m_c, (j + 1) * m_c))
                keep = amp_mask[i, j].astype(jnp.float32)
                masked[part] = (amps[part].astype(jnp.float32) * keep).astype(masked.dtype)

    for s in range(CUTS):
        across(row * CUTS + s).start()

        @pl.when(z < n_z - 1)
        def _():
            upward(row * CUTS + s).start()

        @pl.when(z > 0)
        def _():
            downward(row * CUTS + s).start()

    loads[1].wait()
    mask_amps()

    def each_side(distance, act):
        @pl.when((distance >= 0) & (z - distance >= 0))
        def _():
            act(z - distance, 1)

        @pl.when((distance > 0) & (z + distance < n_z))
        def _():
            act(z + distance, -1)

    def gather_step(d, _):
        def arrive(zz, direction):
            @pl.when(d > 0)
            def _():
                for s in range(CUTS):
                    r = (zz * 2 + x) * CUTS + s
                    across(r).wait_recv()
                    across(r).start()
                    if direction > 0:
                        @pl.when(z < n_z - 1)
                        def _():
                            upward(r).start()
                    else:
                        @pl.when(z > 0)
                        def _():
                            downward(r).start()

        def near(zz, direction):
            for s in range(CUTS):
                multiply(0, (zz * 2 + x) * CUTS + s)

        def other(zz, direction):
            for s in range(CUTS):
                r = (zz * 2 + 1 - x) * CUTS + s
                across(r).wait_recv()
                multiply(0, r)
                if s > 0:
                    combine(0, r - 1)

        def near_sum(zz, direction):
            for s in range(CUTS):
                combine(0, (zz * 2 + x) * CUTS + s)

        def other_sum(zz, direction):
            combine(0, (zz * 2 + 1 - x) * CUTS + CUTS - 1)

        each_side(d, arrive)

        @pl.when(d < n_z)
        def _():
            each_side(d, near)

        each_side(d - 1, near_sum)
        each_side(d - 1, other)
        each_side(d - 2, other_sum)
        return 0

    lax.fori_loop(0, n_z + 2, gather_step, 0)

    loads[2].wait()
    loads[3].wait()
    r_r, r_c = res_mask.shape
    g_r, g_c = rows // r_r, amps.shape[1] // r_c

    def update(step):
        last = step == ITERS - 1
        stores = []
        for h in range(pieces):
            for t in range(1, n_place):
                far_arrival(step, lax.rem(place + t, n_place), h).wait_recv()
            span = min(width, g_c)
            for i in range(r_r):
                for at in range(0, width, span):
                    down = slice(i * g_r, (i + 1) * g_r)
                    along = slice(h * width + at, h * width + at + span)
                    local = slice(at, at + span)
                    keep = res_mask[i, (h * width + at) // g_c].astype(jnp.float32)
                    ladder = hold[place * pieces + h, down, local]
                    for t in range(1, n_place):
                        slot = lax.rem(place + t, n_place) * pieces + h
                        ladder = ladder + far_in[step, slot, down, local].astype(jnp.float32)
                    value = (base[down, along] + ladder) * keep
                    if last:
                        res[down, along] = value
                    amps[down, along] = (
                        amps[down, along].astype(jnp.float32) - inv[down, along] * value
                    ).astype(amps.dtype)
            if last:
                cut = (slice(None), slice(h * width, (h + 1) * width))
                stores += [
                    pltpu.make_async_copy(amps.at[cut], new_hbm.at[cut], store_sem.at[2 * h]),
                    pltpu.make_async_copy(res.at[cut], res_hbm.at[cut], store_sem.at[2 * h + 1]),
                ]
                stores[-2].start()
                stores[-1].start()
        return stores

    stores = update(0)
    for step in range(1, ITERS):
        mask_amps()

        def place_step(t, _):
            there = lax.rem(place + 1 + t, n_place)
            first = there * 2 * pieces
            for h in range(pieces):
                multiply(step, first + (1 - core) * pieces + h)
                multiply(step, first + core * pieces + h)
                if h > 0:
                    combine(step, first + core * pieces + h - 1)
            combine(step, first + core * pieces + pieces - 1)
            return 0

        lax.fori_loop(0, n_place, place_step, 0)
        stores = update(step)

    def drain_lines(zz, _):
        for s in range(CUTS):
            r = (zz * 2 + x) * CUTS + s
            across(r).wait_send()

            @pl.when((zz <= z) & (z < n_z - 1))
            def _():
                upward(r).wait_send()

            @pl.when((zz >= z) & (z > 0))
            def _():
                downward(r).wait_send()

        return 0

    lax.fori_loop(0, n_z, drain_lines, 0)
    for step in range(ITERS):
        def drain_pair(q, _):
            pair_copy(step, q).wait_send()
            return 0

        lax.fori_loop(0, n_place * pieces, drain_pair, 0)
        for t in range(1, n_place):
            for h in range(pieces):
                far_copy(step, lax.rem(place + t, n_place), h).wait_send()
    for store in stores:
        store.wait()


def shards(n_row, n_col, amplitudes, integrals, base_residual, inv_denominators, amp_mask, int_mask, res_mask):
    rows, depth = amplitudes.shape
    width = integrals.shape[1] // CUTS
    blocks = n_row * CUTS
    pieces = depth // width
    slots = (n_col // 2) * pieces
    any_spec = pl.BlockSpec(memory_space=pl.ANY)
    smem = pl.BlockSpec(memory_space=pltpu.SMEM)
    bf16, f32 = jnp.bfloat16, jnp.float32
    dma = pltpu.SemaphoreType.DMA
    return pl.pallas_call(
        functools.partial(kernel, n_row, n_col),
        out_shape=(
            jax.ShapeDtypeStruct(amplitudes.shape, bf16),
            jax.ShapeDtypeStruct(base_residual.shape, f32),
        ),
        in_specs=[smem] * 3 + [any_spec] * 4,
        out_specs=(any_spec, any_spec),
        scratch_shapes=[
            pltpu.VMEM(integrals.shape, bf16),
            pltpu.VMEM((blocks, integrals.shape[0], width), bf16),
            pltpu.VMEM((rows, depth), bf16),
            pltpu.VMEM((rows, depth), bf16),
            pltpu.VMEM((rows, depth), f32),
            pltpu.VMEM((rows, depth), f32),
            pltpu.VMEM((slots, rows, width), f32),
            pltpu.VMEM((ITERS, slots, rows, width), bf16),
            pltpu.VMEM((ITERS, slots, rows, width), bf16),
            pltpu.VMEM((ITERS, slots, rows, width), bf16),
            pltpu.VMEM((ITERS, slots, rows, width), bf16),
            pltpu.VMEM((rows, depth), f32),
            dma((4,)), dma((2 * pieces,)),
            dma((blocks,)), dma((blocks,)), dma((blocks,)), dma((blocks,)),
            dma((ITERS, slots)), dma((ITERS, slots)), dma((ITERS, slots)), dma((ITERS, slots)),
        ],
        compiler_params=pltpu.CompilerParams(
            collective_id=0, has_side_effects=True, vmem_limit_bytes=60 * 2**20
        ),
    )(amp_mask, int_mask.T, res_mask, amplitudes, integrals, base_residual, inv_denominators)


def solution(mesh):
    in_specs = (
        P("row", "col"),
        P("col", "row"),
        P("row", "col"),
        P("row", "col"),
        P("row", "col"),
        P("col", "row"),
        P("row", "col"),
    )
    out_specs = (P("row", "col"), P("row", "col"))
    body = functools.partial(shards, mesh.shape["row"], mesh.shape["col"])
    return jax.shard_map(body, mesh=mesh, in_specs=in_specs, out_specs=out_specs, check_vma=False)
```

```python
import functools

import jax
import jax.numpy as jnp
from jax import lax
from jax.experimental import pallas as pl
from jax.experimental.pallas import tpu as pltpu
from jax.sharding import PartitionSpec as P

ITERS = 2
CUTS = 2
MESH = pl.DeviceIdType.MESH


def kernel(
    n_row, n_col,
    amp_mask, int_mask, res_mask, amps_hbm, ints_hbm, base_hbm, inv_hbm,
    new_hbm, res_hbm,
    raw, ints, amps, masked, base, inv, hold, pair_out, pair_in, far_out, far_in, res,
    load_sem, store_sem, up_sem, down_sem, across_sem, ints_sem,
    pair_send, pair_recv, far_send, far_recv,
):
    row, col = lax.axis_index("row"), lax.axis_index("col")
    z, x = row // 2, row % 2
    place, core = col // 2, col % 2
    n_z, n_place = n_row // 2, n_col // 2
    rows, width = amps.shape[0], ints.shape[2]
    pieces = amps.shape[1] // width

    loads = [
        pltpu.make_async_copy(src, dst, load_sem.at[i])
        for i, (src, dst) in enumerate(
            ((ints_hbm, raw), (amps_hbm, amps), (base_hbm, base), (inv_hbm, inv))
        )
    ]
    for load in loads:
        load.start()

    barrier = pltpu.get_barrier_semaphore()

    def greet(r, c):
        pl.semaphore_signal(barrier, inc=1, device_id=(r, c), device_id_type=MESH)

    greet(row, place * 2 + 1 - core)
    greet(z * 2 + 1 - x, col)

    @pl.when(z > 0)
    def _():
        greet(row - 2, col)

    @pl.when(z < n_z - 1)
    def _():
        greet(row + 2, col)

    for t in range(1, n_place):
        greet(row, lax.rem(place + t, n_place) * 2 + core)

    loads[0].wait()
    t_c, t_r = int_mask.shape
    h_r, h_c = raw.shape[0] // t_r, raw.shape[1] // t_c
    span = min(width, h_c)
    for i in range(t_r):
        for left in range(0, raw.shape[1], span):
            down = slice(i * h_r, (i + 1) * h_r)
            at = left % width
            keep = int_mask[left // h_c, i].astype(jnp.float32)
            ints[row * CUTS + left // width, down, at:at + span] = (
                raw[down, left:left + span].astype(jnp.float32) * keep
            ).astype(ints.dtype)

    peers = n_place + 1 + (z > 0).astype(jnp.int32) + (z < n_z - 1).astype(jnp.int32)
    pl.semaphore_wait(barrier, peers)

    def move(r, send_sem, target):
        return pltpu.make_async_remote_copy(
            src_ref=ints.at[r], dst_ref=ints.at[r], send_sem=send_sem.at[r],
            recv_sem=ints_sem.at[r], device_id=(target, col), device_id_type=MESH,
        )

    def upward(r):
        return move(r, up_sem, row + 2)

    def downward(r):
        return move(r, down_sem, row - 2)

    def across(r):
        return move(r, across_sem, z * 2 + 1 - x)

    def pair_copy(step, q):
        return pltpu.make_async_remote_copy(
            src_ref=pair_out.at[step, q], dst_ref=pair_in.at[step, q],
            send_sem=pair_send.at[step, q], recv_sem=pair_recv.at[step, q],
            device_id=(row, place * 2 + 1 - core), device_id_type=MESH,
        )

    def far_copy(step, owner, h):
        return pltpu.make_async_remote_copy(
            src_ref=far_out.at[step, owner * pieces + h],
            dst_ref=far_in.at[step, place * pieces + h],
            send_sem=far_send.at[step, owner * pieces + h],
            recv_sem=far_recv.at[step, place * pieces + h],
            device_id=(row, owner * 2 + core), device_id_type=MESH,
        )

    def far_arrival(step, source, h):
        return pltpu.make_async_remote_copy(
            src_ref=far_out.at[step, source * pieces + h],
            dst_ref=far_in.at[step, source * pieces + h],
            send_sem=far_send.at[step, source * pieces + h],
            recv_sem=far_recv.at[step, source * pieces + h],
            device_id=(row, source * 2 + core), device_id_type=MESH,
        )

    def multiply(step, r):
        owner = r // pieces
        q = (owner // 2) * pieces + r % pieces
        mine = owner % 2 == core

        @pl.when(mine)
        def _():
            hold[q] = jnp.dot(masked[...], ints[r], preferred_element_type=jnp.float32)

        @pl.when(jnp.logical_not(mine))
        def _():
            pair_out[step, q] = jnp.dot(
                masked[...], ints[r], preferred_element_type=jnp.float32
            ).astype(pair_out.dtype)
            pair_copy(step, q).start()

    def combine(step, r):
        owner = r // pieces
        q = (owner // 2) * pieces + r % pieces

        @pl.when(owner % 2 == core)
        def _():
            pair_copy(step, q).wait_recv()

            @pl.when(owner // 2 == place)
            def _():
                hold[q] = hold[q] + pair_in[step, q].astype(jnp.float32)

            @pl.when(owner // 2 != place)
            def _():
                far_out[step, q] = (hold[q] + pair_in[step, q].astype(jnp.float32)).astype(far_out.dtype)
                far_copy(step, owner // 2, r % pieces).start()

    a_r, a_c = amp_mask.shape
    m_r, m_c = rows // a_r, amps.shape[1] // a_c

    def mask_amps():
        for i in range(a_r):
            for j in range(a_c):
                part = (slice(i * m_r, (i + 1) * m_r), slice(j * m_c, (j + 1) * m_c))
                keep = amp_mask[i, j].astype(jnp.float32)
                masked[part] = (amps[part].astype(jnp.float32) * keep).astype(masked.dtype)

    for s in range(CUTS):
        across(row * CUTS + s).start()

        @pl.when(z < n_z - 1)
        def _():
            upward(row * CUTS + s).start()

        @pl.when(z > 0)
        def _():
            downward(row * CUTS + s).start()

    loads[1].wait()
    mask_amps()

    def each_side(distance, act):
        @pl.when((distance >= 0) & (z - distance >= 0))
        def _():
            act(z - distance, 1)

        @pl.when((distance > 0) & (z + distance < n_z))
        def _():
            act(z + distance, -1)

    def gather_step(d, _):
        def arrive(zz, direction):
            @pl.when(d > 0)
            def _():
                for s in range(CUTS):
                    r = (zz * 2 + x) * CUTS + s
                    across(r).wait_recv()
                    across(r).start()
                    if direction > 0:
                        @pl.when(z < n_z - 1)
                        def _():
                            upward(r).start()
                    else:
                        @pl.when(z > 0)
                        def _():
                            downward(r).start()

        def near(zz, direction):
            for s in range(CUTS):
                multiply(0, (zz * 2 + x) * CUTS + s)

        def other(zz, direction):
            for s in range(CUTS):
                r = (zz * 2 + 1 - x) * CUTS + s
                across(r).wait_recv()
                multiply(0, r)
                if s > 0:
                    combine(0, r - 1)

        def near_sum(zz, direction):
            for s in range(CUTS):
                combine(0, (zz * 2 + x) * CUTS + s)

        def other_sum(zz, direction):
            combine(0, (zz * 2 + 1 - x) * CUTS + CUTS - 1)

        each_side(d, arrive)

        @pl.when(d < n_z)
        def _():
            each_side(d, near)
            each_side(d, near_sum)

        each_side(d - 1, other)
        each_side(d - 1, other_sum)
        return 0

    lax.fori_loop(0, n_z + 1, gather_step, 0)

    loads[2].wait()
    loads[3].wait()
    r_r, r_c = res_mask.shape
    g_r, g_c = rows // r_r, amps.shape[1] // r_c

    def update(step):
        last = step == ITERS - 1
        stores = []
        for h in range(pieces):
            for t in range(1, n_place):
                far_arrival(step, lax.rem(place + t, n_place), h).wait_recv()
            span = min(width, g_c)
            for i in range(r_r):
                for at in range(0, width, span):
                    down = slice(i * g_r, (i + 1) * g_r)
                    along = slice(h * width + at, h * width + at + span)
                    local = slice(at, at + span)
                    keep = res_mask[i, (h * width + at) // g_c].astype(jnp.float32)
                    ladder = hold[place * pieces + h, down, local]
                    for t in range(1, n_place):
                        slot = lax.rem(place + t, n_place) * pieces + h
                        ladder = ladder + far_in[step, slot, down, local].astype(jnp.float32)
                    value = (base[down, along] + ladder) * keep
                    if last:
                        res[down, along] = value
                    amps[down, along] = (
                        amps[down, along].astype(jnp.float32) - inv[down, along] * value
                    ).astype(amps.dtype)
            if last:
                cut = (slice(None), slice(h * width, (h + 1) * width))
                stores += [
                    pltpu.make_async_copy(amps.at[cut], new_hbm.at[cut], store_sem.at[2 * h]),
                    pltpu.make_async_copy(res.at[cut], res_hbm.at[cut], store_sem.at[2 * h + 1]),
                ]
                stores[-2].start()
                stores[-1].start()
        return stores

    stores = update(0)
    for step in range(1, ITERS):
        mask_amps()

        def place_step(t, _):
            there = lax.rem(place + 1 + t, n_place)
            first = there * 2 * pieces
            for h in range(pieces):
                multiply(step, first + (1 - core) * pieces + h)
                multiply(step, first + core * pieces + h)
                if h > 0:
                    combine(step, first + core * pieces + h - 1)
            combine(step, first + core * pieces + pieces - 1)
            return 0

        lax.fori_loop(0, n_place, place_step, 0)
        stores = update(step)

    def drain_lines(zz, _):
        for s in range(CUTS):
            r = (zz * 2 + x) * CUTS + s
            across(r).wait_send()

            @pl.when((zz <= z) & (z < n_z - 1))
            def _():
                upward(r).wait_send()

            @pl.when((zz >= z) & (z > 0))
            def _():
                downward(r).wait_send()

        return 0

    lax.fori_loop(0, n_z, drain_lines, 0)
    for step in range(ITERS):
        def drain_pair(q, _):
            pair_copy(step, q).wait_send()
            return 0

        lax.fori_loop(0, n_place * pieces, drain_pair, 0)
        for t in range(1, n_place):
            for h in range(pieces):
                far_copy(step, lax.rem(place + t, n_place), h).wait_send()
    for store in stores:
        store.wait()


def shards(n_row, n_col, amplitudes, integrals, base_residual, inv_denominators, amp_mask, int_mask, res_mask):
    rows, depth = amplitudes.shape
    width = integrals.shape[1] // CUTS
    blocks = n_row * CUTS
    pieces = depth // width
    slots = (n_col // 2) * pieces
    any_spec = pl.BlockSpec(memory_space=pl.ANY)
    smem = pl.BlockSpec(memory_space=pltpu.SMEM)
    bf16, f32 = jnp.bfloat16, jnp.float32
    dma = pltpu.SemaphoreType.DMA
    return pl.pallas_call(
        functools.partial(kernel, n_row, n_col),
        out_shape=(
            jax.ShapeDtypeStruct(amplitudes.shape, bf16),
            jax.ShapeDtypeStruct(base_residual.shape, f32),
        ),
        in_specs=[smem] * 3 + [any_spec] * 4,
        out_specs=(any_spec, any_spec),
        scratch_shapes=[
            pltpu.VMEM(integrals.shape, bf16),
            pltpu.VMEM((blocks, integrals.shape[0], width), bf16),
            pltpu.VMEM((rows, depth), bf16),
            pltpu.VMEM((rows, depth), bf16),
            pltpu.VMEM((rows, depth), f32),
            pltpu.VMEM((rows, depth), f32),
            pltpu.VMEM((slots, rows, width), f32),
            pltpu.VMEM((ITERS, slots, rows, width), bf16),
            pltpu.VMEM((ITERS, slots, rows, width), bf16),
            pltpu.VMEM((ITERS, slots, rows, width), bf16),
            pltpu.VMEM((ITERS, slots, rows, width), bf16),
            pltpu.VMEM((rows, depth), f32),
            dma((4,)), dma((2 * pieces,)),
            dma((blocks,)), dma((blocks,)), dma((blocks,)), dma((blocks,)),
            dma((ITERS, slots)), dma((ITERS, slots)), dma((ITERS, slots)), dma((ITERS, slots)),
        ],
        compiler_params=pltpu.CompilerParams(
            collective_id=0, has_side_effects=True, vmem_limit_bytes=60 * 2**20
        ),
    )(amp_mask, int_mask.T, res_mask, amplitudes, integrals, base_residual, inv_denominators)


def solution(mesh):
    in_specs = (
        P("row", "col"),
        P("col", "row"),
        P("row", "col"),
        P("row", "col"),
        P("row", "col"),
        P("col", "row"),
        P("row", "col"),
    )
    out_specs = (P("row", "col"), P("row", "col"))
    body = functools.partial(shards, mesh.shape["row"], mesh.shape["col"])
    return jax.shard_map(body, mesh=mesh, in_specs=in_specs, out_specs=out_specs, check_vma=False)
```
